32 devices in a mesh: dp: 4 (over z), phase: 2 (over x), ctx: 4 (over y, core).
Axes of the slice: x: 2, y: 2, z: 4, core: 2. Of those that a mesh axis runs over, the one named last changes fastest.
Arguments:
- queries: bfloat16 [4, 1024, 2048], P('dp', 'ctx', 'phase'), may hold values from -6 to 6
- keys: bfloat16 [4, 1024, 256], P('dp', 'ctx', 'phase'), may hold values from -6 to 6
- values: bfloat16 [4, 1024, 256], P('dp', 'ctx', 'phase'), may hold values from -6 to 6
- segment_ids: int32 [4, 1024], P('dp', 'ctx'), may hold values from 0 to 7, never falling along the last dimension, each value on 1 to 256 neighbouring positions
- span_ids: int32 [4, 1024], P('dp', 'ctx'), may hold values from 0 to 2, as said below
- readout: float32 [2048], P('phase'), may hold values from -6 to 6
Outputs:
- attended: bfloat16 [4, 1024, 2048], P('dp', 'ctx', 'phase')
- span_scores: float32 [4, 2], P('dp')
- pair_loss: float32 [], replicated
The draws below stay inside these ranges and needn't reach their ends.
Inputs may be any that keep to these rules, and one draw needn't show every extreme that they name: `segment_ids`: segment ids never fall along a sequence; each segment covers at most 256 positions, and some segment covers exactly that many. `span_ids`: positions labelled 1 form one contiguous run, and positions labelled 2 form one later contiguous run.
All inputs are finite; a program needn't handle non-finite values.
Results may differ from the reference program's by a relative error of at most 0.0036.
Values may be sent and summed in bfloat16 or wider, within the bound.
A program may use at most 128 MiB of HBM per device.

```python
import math
import jax
import jax.numpy as jnp
import numpy as np
from jax import lax

HD = 128
QPK = 8
KVH = 2
HEADS = 16
SEQ = 1024
SEQS = 4


def plant_layout(key):
    layout_key = jax.random.fold_in(key, 7177)
    pick_key, sign_key = jax.random.split(layout_key)
    quarter = SEQ // 4
    offsets = jax.random.randint(pick_key, (SEQS, 4), 2, quarter)
    points = offsets + (jnp.arange(4) * quarter)[None, :]
    position = jnp.arange(SEQ)
    planted = jnp.any(position[None, :, None] == points[:, None, :], axis=-1)
    preceding = jnp.any(position[None, :, None] + 1 == points[:, None, :], axis=-1)
    coins = jax.random.bernoulli(sign_key, 0.5, (SEQS, SEQ, KVH, HD))
    sign_field = jnp.where(coins, 1.0, -1.0).astype(jnp.float32)
    return (planted, preceding, sign_field)


def draw_queries(key, part):
    planted, preceding, sign_field = plant_layout(key)
    noise_key = jax.random.fold_in(key, 11)
    level_key = jax.random.fold_in(key, 53)
    full_shape = (SEQS, SEQ, KVH, QPK, HD)
    noise_field = jnp.clip(jax.random.normal(noise_key, full_shape, jnp.float32), -6.0, 6.0)
    levels = jax.random.randint(level_key, (SEQS, SEQ, KVH, QPK, 1), 0, 4).astype(jnp.float32)
    strength = 4.5 + 0.5 * levels
    aligned = strength * sign_field[:, :, :, None, :]
    result = jnp.where(planted[:, :, None, None, None], aligned, noise_field)
    return result.reshape(SEQS, SEQ, HEADS * HD).astype(jnp.bfloat16)


def draw_keys(key, part):
    planted, preceding, sign_field = plant_layout(key)
    noise_key = jax.random.fold_in(key, 29)
    full_shape = (SEQS, SEQ, KVH, HD)
    noise_field = jnp.clip(jax.random.normal(noise_key, full_shape, jnp.float32), -6.0, 6.0)
    following = jnp.roll(sign_field, -1, axis=1)
    lowered = jnp.where(jnp.arange(HD) < max(1, HD // 64), 1.75, 3.5).astype(jnp.float32)
    near_copy = following * lowered[None, None, None, :]
    result = jnp.where(planted[:, :, None, None], 3.5 * sign_field, jnp.where(preceding[:, :, None, None], near_copy, noise_field))
    return result.reshape(SEQS, SEQ, KVH * HD).astype(jnp.bfloat16)


def draw_span_ids(key, part):
    first_key, second_key, third_key, fourth_key = jax.random.split(jax.random.fold_in(key, 97), 4)
    position = jnp.arange(SEQ)[None, :]
    chosen_start = jax.random.randint(first_key, (SEQS, 1), SEQ // 16, SEQ // 8)
    chosen_length = jax.random.randint(second_key, (SEQS, 1), SEQ // 4, 3 * SEQ // 8 + 1)
    reject_start = SEQ // 2 + jax.random.randint(third_key, (SEQS, 1), SEQ // 16, SEQ // 8)
    reject_length = jax.random.randint(fourth_key, (SEQS, 1), SEQ // 4, 3 * SEQ // 8 + 1)
    chosen = (position >= chosen_start) & (position < chosen_start + chosen_length)
    reject = (position >= reject_start) & (position < reject_start + reject_length)
    return jnp.where(chosen, 1, jnp.where(reject, 2, 0)).astype(jnp.int32)


def block_levels(rng, extent, shards, least, top_value):
    gain, own = 1.0, jax.random.fold_in(rng, 6)
    for axis_at, parts in shards:
        steps = jnp.exp(jax.random.uniform(jax.random.fold_in(own, axis_at), (parts,), jnp.float32, least / len(shards), top_value / len(shards)))
        gain = gain * jnp.repeat(steps, extent[axis_at] // parts).reshape([-1 if axis == axis_at else 1 for axis in range(len(extent))])
    return gain


def length_profile(count, total, bound, lean):
    loads = [(1 << 20) // math.isqrt(grade ** lean) + 1 for grade in range(2, count + 1)]
    rest, given = total - bound - (count - 1), [1] * (count - 1)
    while rest > 0:
        free = [i for i in range(count - 1) if given[i] < bound]
        mass, budget = sum([loads[i] for i in free]), rest
        for i in free:
            addition = min(bound - given[i], max(1, budget * loads[i] // mass), rest)
            given[i] = given[i] + addition
            rest = rest - addition
    return np.array([bound] + given)


def uneven_parts(rng, count, total, most, slope):
    if count == 2:
        one = jax.random.randint(rng, (), max(1, total - most), min(most, total - 1) + 1)
        return jnp.stack([one, total - one])
    lengths = jnp.asarray(length_profile(count, total, most, slope), jnp.int32)
    couples = (count - 1) // 2
    donor, taker = lengths[1:1 + 2 * couples:2], lengths[2:2 + 2 * couples:2]
    room = jnp.minimum(donor - 1, most - taker)
    shifted = jax.random.randint(jax.random.fold_in(rng, 1), (couples,), 0, 1 << 20) % (room + 1)
    lengths = lengths.at[1:1 + 2 * couples:2].set(donor - shifted).at[2:2 + 2 * couples:2].set(taker + shifted)
    return lengths[jax.random.permutation(jax.random.fold_in(rng, 2), count)]


def normal_values(rng, dims, scale, limit, pieces=(), dtype=jnp.bfloat16):
    values = jax.random.normal(rng, dims, jnp.float32) * scale
    if len(pieces) > 0:
        values = block_levels(rng, dims, pieces, -0.22, 0.18) * values
    return jnp.clip(values, min=-limit, max=limit).astype(dtype)


def setup_inputs(seed: int = 0) -> dict:
    splits = jax.random.split(jax.random.key(seed), 7)
    queries = draw_queries(jax.random.fold_in(splits[6], 71), 0)
    keys = draw_keys(jax.random.fold_in(splits[6], 71), 0)
    values = normal_values(splits[2], (SEQS, SEQ, KVH * HD), 1.0, 6.0, ((0, 4), (1, 4), (2, 2)))
    segment_ids = jax.vmap(lambda own: jnp.searchsorted(jnp.cumsum(uneven_parts(own, 8, SEQ, SEQ // 4, 2)), jnp.arange(SEQ), side="right"))(jax.random.split(splits[3], SEQS)).reshape((SEQS, SEQ)).astype(jnp.int32)
    span_ids = draw_span_ids(jax.random.fold_in(splits[6], 71), 0)
    readout = normal_values(splits[5], (HEADS * HD,), 1.0, 6.0, ((0, 2),), jnp.float32)
    return dict(queries=queries, keys=keys, values=values, segment_ids=segment_ids, span_ids=span_ids, readout=readout)


def one_seq(args):
    qs, ks, vs, segs, spans, readout = args
    pos = jnp.arange(SEQ)
    rows = 512 if SEQ % 512 == 0 else SEQ
    qb = qs.reshape(SEQ // rows, rows, HEADS, HD)

    def block(item):
        qblk, start = item
        qpos = start + jnp.arange(rows)
        qseg = lax.dynamic_slice_in_dim(segs, start, rows)
        allow = (pos[None, :] <= qpos[:, None]) & (segs[None, :] == qseg[:, None])
        outs = []
        for g in range(KVH):
            qh = qblk[:, g * QPK:(g + 1) * QPK, :].astype(jnp.float32)
            kh = ks[:, g * HD:(g + 1) * HD].astype(jnp.float32)
            vh = vs[:, g * HD:(g + 1) * HD].astype(jnp.float32)
            sc = jnp.einsum('ihd,jd->hij', qh, kh) / jnp.sqrt(jnp.float32(HD))
            sc = jnp.where(allow[None], sc, jnp.float32(-1e+30))
            top = lax.optimization_barrier(jnp.max(sc, axis=-1, keepdims=True))
            prob = jnp.where(allow[None], jnp.exp(sc - top), 0.0)
            total = lax.optimization_barrier(jnp.sum(prob, axis=-1))
            wts = prob.astype(jnp.bfloat16).astype(jnp.float32)
            acc = jnp.einsum('hij,jd->ihd', wts, vh)
            outs.append(acc / jnp.transpose(total)[:, :, None])
        return jnp.concatenate(outs, axis=1).reshape(rows, HEADS * HD)
    starts = (jnp.arange(SEQ // rows) * rows).astype(jnp.int32)
    full = lax.map(block, (qb, starts)).reshape(SEQ, HEADS * HD)
    score = lax.optimization_barrier(jnp.sum(full * readout[None, :], axis=1))
    chosen = jnp.sum(jnp.where(spans == 1, score, 0.0)) / 64.0
    reject = jnp.sum(jnp.where(spans == 2, score, 0.0)) / 64.0
    return (full.astype(jnp.bfloat16), jnp.stack([chosen, reject]))

def reference(queries, keys, values, segment_ids, span_ids, readout):
    reps = jnp.broadcast_to(readout, (SEQS, HEADS * HD))
    attended, span_scores = lax.map(one_seq, (queries, keys, values, segment_ids, span_ids, reps))
    pair_loss = jnp.mean(jax.nn.softplus(-(span_scores[:, 0] - span_scores[:, 1])))
    return (attended, span_scores, pair_loss)
```

```python
import functools
import math

import jax
import jax.numpy as jnp
from jax import lax
from jax.experimental import pallas as pl
from jax.experimental.pallas import tpu as pltpu
from jax.sharding import PartitionSpec as P

MESH = pl.DeviceIdType.MESH
NT = (((1,), (1,)), ((), ()))
NN = (((1,), (0,)), ((), ()))
OFF = -1e30


def fused(
    sizes,
    q_hbm, k_hbm, v_hbm, seg_hbm, span_hbm, read_hbm,
    att_hbm, spans_ref, loss_ref,
    qv, kv, vv, segv, spanv, readv, kr, vr, sr, near, bias, attv, sums, terms,
    load_sem, out_sem, ksend, vsend, ssend, krecv, vrecv, srecv,
    asend, arecv, bsend, brecv,
):
    dp, phase, ctx, steps = sizes
    at_dp, at_phase, here = lax.axis_index("dp"), lax.axis_index("phase"), lax.axis_index("ctx")
    tok, head_dim = kv.shape
    heads = qv.shape[1] // head_dim
    group = phase * ctx
    mine = at_phase * ctx + here

    def in_group(by):
        other = lax.rem(mine + by, group)
        return {"dp": at_dp, "phase": other // ctx, "ctx": lax.rem(other, ctx)}

    def in_dp(by):
        return {"dp": lax.rem(at_dp + by, dp), "phase": at_phase, "ctx": here}

    barrier = pltpu.get_barrier_semaphore()
    for by in range(1, group):
        pl.semaphore_signal(barrier, inc=1, device_id=in_group(by), device_id_type=MESH)
    for by in range(1, dp):
        pl.semaphore_signal(barrier, inc=1, device_id=in_dp(by), device_id_type=MESH)

    loads = [
        pltpu.make_async_copy(src, dst, load_sem.at[i])
        for i, (src, dst) in enumerate(
            [(k_hbm, kv), (q_hbm, qv), (v_hbm, vv), (seg_hbm, segv), (span_hbm, spanv), (read_hbm, readv)]
        )
    ]
    for load in loads:
        load.start()

    for step in range(1, steps + 1):

        @pl.when(here < step)
        def _():
            kr[step - 1] = jnp.zeros((tok, head_dim), kr.dtype)
            vr[step - 1] = jnp.zeros((tok, head_dim), vr.dtype)
            sr[step - 1] = jnp.full((1, tok), -1, jnp.int32)

    pl.semaphore_wait(barrier, group + dp - 2)

    def halo(step):
        i = step - 1
        target = {"dp": at_dp, "phase": at_phase, "ctx": lax.rem(here + step, ctx)}
        return [
            pltpu.make_async_remote_copy(
                src_ref=src, dst_ref=dst.at[i], send_sem=ss.at[i], recv_sem=rs.at[i],
                device_id=target, device_id_type=MESH,
            )
            for src, dst, ss, rs in (
                (seg_hbm, sr, ssend, srecv), (k_hbm, kr, ksend, krecv), (v_hbm, vr, vsend, vrecv)
            )
        ]

    for step in range(1, steps + 1):

        @pl.when(here + step < ctx)
        def _():
            for copy in halo(step):
                copy.start()

    loads[0].wait()
    loads[1].wait()

    def query(h):
        return qv[:, h * head_dim:(h + 1) * head_dim]

    for h in range(heads):
        near[h] = lax.dot_general(kv[...], query(h), NT, preferred_element_type=jnp.float32)

    for load in loads[2:]:
        load.wait()

    qseg = segv[...].astype(jnp.float32)

    def down(row):
        wide = jnp.broadcast_to(row, (head_dim, tok))
        tall = jnp.transpose(wide)
        return jnp.concatenate([tall] * (tok // head_dim), axis=1)

    own_seg = down(qseg)
    vt_own = jnp.transpose(vv[...])
    reads = jnp.transpose(readv[...])
    tri = lax.broadcasted_iota(jnp.int32, (tok, tok), 0) <= lax.broadcasted_iota(jnp.int32, (tok, tok), 1)

    for step in range(1, steps + 1):

        @pl.when(here >= step)
        def _():
            for copy in halo(step):
                copy.wait_recv()

    for step in range(1, steps + 1):
        far = down(sr[step - 1].astype(jnp.float32))
        if step == steps:
            far = jnp.where(tri, own_seg, far)
        bias[step - 1] = jnp.where(far == qseg, 0.0, OFF)

    vts = [jnp.transpose(vr[s]) for s in range(steps)]
    rate = math.log2(math.e) / math.sqrt(head_dim)
    outs = []
    held = jnp.zeros((head_dim, tok), jnp.float32)
    for h in range(heads):
        qh = query(h)
        scores = []
        for s in range(steps):
            sc = lax.dot_general(kr[s], qh, NT, preferred_element_type=jnp.float32)
            if s == steps - 1:
                sc = jnp.where(tri, near[h], sc)
            scores.append(sc + bias[s])
        top = functools.reduce(jnp.maximum, [jnp.max(sc, axis=0, keepdims=True) for sc in scores])
        probs = [jnp.exp2((sc - top) * rate) for sc in scores]
        total = sum(jnp.sum(p, axis=0, keepdims=True) for p in probs)
        acc = lax.dot_general(
            vt_own, jnp.where(tri, probs[-1], 0.0).astype(jnp.bfloat16), NN, preferred_element_type=jnp.float32
        )
        for s in range(steps):
            p = probs[s] if s < steps - 1 else jnp.where(tri, 0.0, probs[s])
            acc += lax.dot_general(vts[s], p.astype(jnp.bfloat16), NN, preferred_element_type=jnp.float32)
        full = acc / total
        held += full * reads[:, h:h + 1]
        attv[:, h * head_dim:(h + 1) * head_dim] = jnp.transpose(full).astype(attv.dtype)
    out = pltpu.make_async_copy(attv, att_hbm, out_sem)
    out.start()

    score = jnp.sum(held, axis=0, keepdims=True)
    spans = spanv[...]
    lane = lax.broadcasted_iota(jnp.int32, (1, 128), 1)
    chosen = jnp.sum(jnp.where(spans == 1, score, 0.0), axis=1, keepdims=True)
    reject = jnp.sum(jnp.where(spans == 2, score, 0.0), axis=1, keepdims=True)
    sums[mine] = jnp.where(lane == 0, chosen, jnp.where(lane == 1, reject, 0.0))
    acopies = [
        pltpu.make_async_remote_copy(
            src_ref=sums.at[mine], dst_ref=sums.at[mine], send_sem=asend, recv_sem=arecv,
            device_id=in_group(by), device_id_type=MESH,
        )
        for by in range(1, group)
    ]
    for copy in acopies:
        copy.start()
    others = sums.at[pl.ds(0, group - 1)]
    pltpu.make_async_copy(others, others, arecv).wait()
    pair = jnp.sum(sums[...], axis=0) / 64.0
    spans_ref[...] = pair[:, :2]
    gap = pair[:, 1:2] - pair[:, 0:1]
    term = jnp.maximum(gap, 0.0) + jnp.log1p(jnp.exp(-jnp.abs(gap)))
    terms[at_dp] = jnp.broadcast_to(term, (1, 128))
    bcopies = [
        pltpu.make_async_remote_copy(
            src_ref=terms.at[at_dp], dst_ref=terms.at[at_dp], send_sem=bsend, recv_sem=brecv,
            device_id=in_dp(by), device_id_type=MESH,
        )
        for by in range(1, dp)
    ]
    for copy in bcopies:
        copy.start()
    others_b = terms.at[pl.ds(0, dp - 1)]
    pltpu.make_async_copy(others_b, others_b, brecv).wait()
    loss_ref[...] = (jnp.sum(terms[...], axis=0) / dp)[:, :1]

    pltpu.make_async_copy(others, others, asend).wait()
    pltpu.make_async_copy(others_b, others_b, bsend).wait()
    for step in range(1, steps + 1):

        @pl.when(here + step < ctx)
        def _():
            for copy in halo(step):
                copy.wait_send()

    out.wait()


def solution(mesh):
    dp, phase, ctx = mesh.shape["dp"], mesh.shape["phase"], mesh.shape["ctx"]
    steps = ctx // 4

    def per_device(queries, keys, values, segment_ids, span_ids, readout):
        tok, head_dim = keys.shape[1:]
        width = queries.shape[2]
        heads = width // head_dim
        any_spec = pl.BlockSpec(memory_space=pl.ANY)
        vmem = pl.BlockSpec(memory_space=pltpu.VMEM)
        dma = pltpu.SemaphoreType.DMA
        att, spans, loss = pl.pallas_call(
            functools.partial(fused, (dp, phase, ctx, steps)),
            out_shape=(
                jax.ShapeDtypeStruct((tok, width), jnp.bfloat16),
                jax.ShapeDtypeStruct((1, 2), jnp.float32),
                jax.ShapeDtypeStruct((1, 1), jnp.float32),
            ),
            in_specs=[any_spec] * 6,
            out_specs=(any_spec, vmem, vmem),
            scratch_shapes=[
                pltpu.VMEM((tok, width), jnp.bfloat16),
                pltpu.VMEM((tok, head_dim), jnp.bfloat16),
                pltpu.VMEM((tok, head_dim), jnp.bfloat16),
                pltpu.VMEM((1, tok), jnp.int32),
                pltpu.VMEM((1, tok), jnp.int32),
                pltpu.VMEM((heads, head_dim), jnp.float32),
                pltpu.VMEM((steps, tok, head_dim), jnp.bfloat16),
                pltpu.VMEM((steps, tok, head_dim), jnp.bfloat16),
                pltpu.VMEM((steps, 1, tok), jnp.int32),
                pltpu.VMEM((heads, tok, tok), jnp.float32),
                pltpu.VMEM((steps, tok, tok), jnp.float32),
                pltpu.VMEM((tok, width), jnp.bfloat16),
                pltpu.VMEM((phase * ctx, 1, 128), jnp.float32),
                pltpu.VMEM((dp, 1, 128), jnp.float32),
                dma((6,)),
                dma,
                dma((steps,)), dma((steps,)), dma((steps,)),
                dma((steps,)), dma((steps,)), dma((steps,)),
                dma, dma, dma, dma,
            ],
            compiler_params=pltpu.CompilerParams(
                collective_id=0, has_side_effects=True, vmem_limit_bytes=32 * 1024 * 1024
            ),
            cost_estimate=pl.CostEstimate(
                flops=8 * heads * tok * tok * head_dim, bytes_accessed=4 * tok * width + 4 * tok * head_dim,
                transcendentals=heads * tok * tok,
            ),
        )(queries[0], keys[0], values[0], segment_ids, span_ids, readout.reshape(heads, head_dim))
        return att[None], spans, loss.reshape(())

    in_specs = (
        P("dp", "ctx", "phase"),
        P("dp", "ctx", "phase"),
        P("dp", "ctx", "phase"),
        P("dp", "ctx"),
        P("dp", "ctx"),
        P("phase"),
    )
    out_specs = (P("dp", "ctx", "phase"), P("dp", None), P())
    return jax.shard_map(
        per_device, mesh=mesh, in_specs=in_specs, out_specs=out_specs, check_vma=False
    )
```

```python
import functools
import math

import jax
import jax.numpy as jnp
from jax import lax
from jax.experimental import pallas as pl
from jax.experimental.pallas import tpu as pltpu
from jax.sharding import PartitionSpec as P

MESH = pl.DeviceIdType.MESH
NT = (((1,), (1,)), ((), ()))
NN = (((1,), (0,)), ((), ()))
OFF = -1e30


def fused(
    sizes,
    q_hbm, k_hbm, v_hbm, seg_hbm, span_hbm, read_hbm,
    att_ref, tot_ref,
    qv, kv, vv, segv, spanv, readv, kr, vr, sr, near, bias, sums, terms,
    load_sem, ksend, vsend, ssend, krecv, vrecv, srecv,
    asend, arecv, bsend, brecv,
):
    dp, phase, ctx, steps, flat = sizes
    at_dp, at_phase, here = lax.axis_index("dp"), lax.axis_index("phase"), lax.axis_index("ctx")
    tok, head_dim = kv.shape
    heads = qv.shape[1] // head_dim
    group = phase * ctx
    mine = at_phase * ctx + here

    def away(z, x, y):
        return {"dp": along_dp[z], "phase": along_phase[x], "ctx": along_ctx[y]}

    along_dp = [at_dp] + [lax.rem(at_dp + by, dp) for by in range(1, dp)]
    along_phase = [at_phase] + [lax.rem(at_phase + by, phase) for by in range(1, phase)]
    along_ctx = [here] + [lax.rem(here + by, ctx) for by in range(1, ctx)]
    in_group = [(0, x, y) for x in range(phase) for y in range(ctx)][1:]
    in_dp = [(z, 0, 0) for z in range(1, dp)]
    if flat:
        in_dp = [(z, x, y) for z in range(1, dp) for x in range(phase) for y in range(ctx)]

    barrier = pltpu.get_barrier_semaphore()
    for by in in_dp[::-1] + in_group:
        pl.semaphore_signal(barrier, inc=1, device_id=away(*by), device_id_type=MESH)

    loads = [
        pltpu.make_async_copy(src, dst, load_sem.at[i])
        for i, (src, dst) in enumerate(
            [(k_hbm, kv), (q_hbm, qv), (v_hbm, vv), (seg_hbm, segv), (span_hbm, spanv), (read_hbm, readv)]
        )
    ]
    for load in loads:
        load.start()

    for step in range(1, steps + 1):

        @pl.when(here < step)
        def _():
            kr[step - 1] = jnp.zeros((tok, head_dim), kr.dtype)
            vr[step - 1] = jnp.zeros((tok, head_dim), vr.dtype)
            sr[step - 1] = jnp.full((1, tok), -1, jnp.int32)

    pl.semaphore_wait(barrier, len(in_group) + len(in_dp))

    def halo(step):
        i = step - 1
        target = {"dp": at_dp, "phase": at_phase, "ctx": lax.rem(here + step, ctx)}
        return [
            pltpu.make_async_remote_copy(
                src_ref=src, dst_ref=dst.at[i], send_sem=ss.at[i], recv_sem=rs.at[i],
                device_id=target, device_id_type=MESH,
            )
            for src, dst, ss, rs in (
                (seg_hbm, sr, ssend, srecv), (k_hbm, kr, ksend, krecv), (v_hbm, vr, vsend, vrecv)
            )
        ]

    for step in range(1, steps + 1):

        @pl.when(here + step < ctx)
        def _():
            for copy in halo(step):
                copy.start()

    loads[0].wait()
    loads[1].wait()

    def query(h):
        return qv[:, h * head_dim:(h + 1) * head_dim]

    for h in range(heads):
        near[h] = lax.dot_general(kv[...], query(h), NT, preferred_element_type=jnp.float32)

    for load in loads[2:]:
        load.wait()

    qseg = segv[...].astype(jnp.float32)

    def down(row):
        wide = jnp.broadcast_to(row, (head_dim, tok))
        tall = jnp.transpose(wide)
        return jnp.concatenate([tall] * (tok // head_dim), axis=1)

    own_seg = down(qseg)
    vt_own = jnp.transpose(vv[...])
    reads = jnp.transpose(readv[...])
    tri = lax.broadcasted_iota(jnp.int32, (tok, tok), 0) <= lax.broadcasted_iota(jnp.int32, (tok, tok), 1)

    for step in range(1, steps + 1):

        @pl.when(here >= step)
        def _():
            for copy in halo(step):
                copy.wait_recv()

    for step in range(1, steps + 1):
        far = down(sr[step - 1].astype(jnp.float32))
        if step == steps:
            far = jnp.where(tri, own_seg, far)
        bias[step - 1] = jnp.where(far == qseg, 0.0, OFF)

    vts = [jnp.transpose(vr[s]) for s in range(steps)]
    rate = math.log2(math.e) / math.sqrt(head_dim)
    outs = []
    held = jnp.zeros((head_dim, tok), jnp.float32)
    for h in range(heads):
        qh = query(h)
        scores = []
        for s in range(steps):
            sc = lax.dot_general(kr[s], qh, NT, preferred_element_type=jnp.float32)
            if s == steps - 1:
                sc = jnp.where(tri, near[h], sc)
            scores.append(sc + bias[s])
        top = functools.reduce(jnp.maximum, [jnp.max(sc, axis=0, keepdims=True) for sc in scores])
        probs = [jnp.exp2((sc - top) * rate) for sc in scores]
        total = sum(jnp.sum(p, axis=0, keepdims=True) for p in probs)
        acc = lax.dot_general(
            vt_own, jnp.where(tri, probs[-1], 0.0).astype(jnp.bfloat16), NN, preferred_element_type=jnp.float32
        )
        for s in range(steps):
            p = probs[s] if s < steps - 1 else jnp.where(tri, 0.0, probs[s])
            acc += lax.dot_general(vts[s], p.astype(jnp.bfloat16), NN, preferred_element_type=jnp.float32)
        full = acc / total
        held += full * reads[:, h:h + 1]
        att_ref[:, h * head_dim:(h + 1) * head_dim] = jnp.transpose(full).astype(att_ref.dtype)

    score = jnp.sum(held, axis=0, keepdims=True)
    spans = spanv[...]
    lane = lax.broadcasted_iota(jnp.int32, (1, 128), 1)
    chosen = jnp.sum(jnp.where(spans == 1, score, 0.0), axis=1, keepdims=True)
    reject = jnp.sum(jnp.where(spans == 2, score, 0.0), axis=1, keepdims=True)
    row = jnp.where(lane == 0, chosen, jnp.where(lane == 1, reject, 0.0))

    def spread(slots, slot, targets, send_sem, recv_sem):
        for by in targets:
            pltpu.make_async_remote_copy(
                src_ref=slots.at[slot], dst_ref=slots.at[slot], send_sem=send_sem, recv_sem=recv_sem,
                device_id=away(*by), device_id_type=MESH,
            ).start()
        rest = slots.at[pl.ds(0, len(targets))]
        pltpu.make_async_copy(rest, rest, recv_sem).wait()
        return pltpu.make_async_copy(rest, rest, send_sem)

    if flat:
        slot = at_dp * group + mine
        sums[slot] = row
        sent = [spread(sums, slot, in_dp[::-1] + in_group, asend, arecv)]
        for z in range(dp):
            tot_ref[z] = jnp.sum(sums[z * group:(z + 1) * group], axis=0) / 64.0
    else:
        sums[mine] = row
        sent = [spread(sums, mine, in_group, asend, arecv)]
        terms[at_dp] = jnp.sum(sums[...], axis=0) / 64.0
        sent.append(spread(terms, at_dp, in_dp, bsend, brecv))
        tot_ref[...] = terms[...]
    for copy in sent:
        copy.wait()
    for step in range(1, steps + 1):

        @pl.when(here + step < ctx)
        def _():
            for copy in halo(step):
                copy.wait_send()


def finish(att_ref, tot_ref, out_ref, spans_ref, loss_ref, sem):
    copy = pltpu.make_async_copy(att_ref, out_ref, sem)
    copy.start()
    tot = tot_ref[...]
    gap = tot[:, :, 1:2] - tot[:, :, 0:1]
    term = jnp.maximum(gap, 0.0) + jnp.log1p(jnp.exp(-jnp.abs(gap)))
    loss_ref[...] = jnp.sum(term, axis=0) / tot.shape[0]
    spans_ref[...] = tot_ref[lax.axis_index("dp")][:, :2]
    copy.wait()


def solution(mesh):
    dp, phase, ctx = mesh.shape["dp"], mesh.shape["phase"], mesh.shape["ctx"]
    steps = ctx // 4
    flat = dp * phase * ctx <= 64

    def per_device(queries, keys, values, segment_ids, span_ids, readout):
        tok, head_dim = keys.shape[1:]
        width = queries.shape[2]
        heads = width // head_dim
        any_spec = pl.BlockSpec(memory_space=pl.ANY)
        slots = dp * phase * ctx if flat else phase * ctx
        vmem = pl.BlockSpec(memory_space=pltpu.VMEM)
        dma = pltpu.SemaphoreType.DMA
        att, tot = pl.pallas_call(
            functools.partial(fused, (dp, phase, ctx, steps, flat)),
            out_shape=(
                jax.ShapeDtypeStruct((tok, width), jnp.bfloat16),
                jax.ShapeDtypeStruct((dp, 1, 128), jnp.float32),
            ),
            in_specs=[any_spec] * 6,
            out_specs=(vmem, vmem),
            scratch_shapes=[
                pltpu.VMEM((tok, width), jnp.bfloat16),
                pltpu.VMEM((tok, head_dim), jnp.bfloat16),
                pltpu.VMEM((tok, head_dim), jnp.bfloat16),
                pltpu.VMEM((1, tok), jnp.int32),
                pltpu.VMEM((1, tok), jnp.int32),
                pltpu.VMEM((heads, head_dim), jnp.float32),
                pltpu.VMEM((steps, tok, head_dim), jnp.bfloat16),
                pltpu.VMEM((steps, tok, head_dim), jnp.bfloat16),
                pltpu.VMEM((steps, 1, tok), jnp.int32),
                pltpu.VMEM((heads, tok, tok), jnp.float32),
                pltpu.VMEM((steps, tok, tok), jnp.float32),
                pltpu.VMEM((slots, 1, 128), jnp.float32),
                pltpu.VMEM((dp, 1, 128), jnp.float32),
                dma((6,)),
                dma((steps,)), dma((steps,)), dma((steps,)),
                dma((steps,)), dma((steps,)), dma((steps,)),
                dma, dma, dma, dma,
            ],
            compiler_params=pltpu.CompilerParams(
                collective_id=0, has_side_effects=True, vmem_limit_bytes=32 * 1024 * 1024
            ),
            cost_estimate=pl.CostEstimate(
                flops=8 * heads * tok * tok * head_dim, bytes_accessed=4 * tok * width + 4 * tok * head_dim,
                transcendentals=heads * tok * tok,
            ),
        )(*[
            pltpu.with_memory_space_constraint(a, pltpu.HBM)
            for a in (queries[0], keys[0], values[0], segment_ids, span_ids, readout.reshape(heads, head_dim))
        ])
        att, spans, loss = pl.pallas_call(
            finish,
            out_shape=(
                jax.ShapeDtypeStruct((tok, width), jnp.bfloat16),
                jax.ShapeDtypeStruct((1, 2), jnp.float32),
                jax.ShapeDtypeStruct((1, 1), jnp.float32),
            ),
            in_specs=[any_spec, vmem],
            out_specs=(any_spec, vmem, vmem),
            scratch_shapes=[dma],
            compiler_params=pltpu.CompilerParams(vmem_limit_bytes=1024 * 1024),
        )(att, tot)
        return att[None], spans, loss.reshape(())

    in_specs = (
        P("dp", "ctx", "phase"),
        P("dp", "ctx", "phase"),
        P("dp", "ctx", "phase"),
        P("dp", "ctx"),
        P("dp", "ctx"),
        P("phase"),
    )
    out_specs = (P("dp", "ctx", "phase"), P("dp", None), P())
    return jax.shard_map(
        per_device, mesh=mesh, in_specs=in_specs, out_specs=out_specs, check_vma=False
    )
```

```python
import functools
import math

import jax
import jax.numpy as jnp
from jax import lax
from jax.experimental import pallas as pl
from jax.experimental.pallas import tpu as pltpu
from jax.sharding import PartitionSpec as P

MESH = pl.DeviceIdType.MESH
NT = (((1,), (1,)), ((), ()))
NN = (((1,), (0,)), ((), ()))
OFF = -1e30


def fused(
    sizes,
    q_hbm, k_hbm, v_hbm, seg_hbm, span_hbm, read_hbm,
    att_ref, tot_ref,
    qv, kv, vv, segv, spanv, readv, kr, vr, sr, near, bias, wts, sums, terms,
    load_sem, ksend, vsend, ssend, krecv, vrecv, srecv,
    asend, arecv, bsend, brecv,
):
    dp, phase, ctx, steps, flat = sizes
    at_dp, at_phase, here = lax.axis_index("dp"), lax.axis_index("phase"), lax.axis_index("ctx")
    tok, head_dim = kv.shape
    heads = qv.shape[1] // head_dim
    group = phase * ctx
    mine = at_phase * ctx + here

    def away(z, x, y):
        return {"dp": along_dp[z], "phase": along_phase[x], "ctx": along_ctx[y]}

    along_dp = [at_dp] + [lax.rem(at_dp + by, dp) for by in range(1, dp)]
    along_phase = [at_phase] + [lax.rem(at_phase + by, phase) for by in range(1, phase)]
    along_ctx = [here] + [lax.rem(here + by, ctx) for by in range(1, ctx)]
    in_group = [(0, x, y) for x in range(phase) for y in range(ctx)][1:]
    in_dp = [(z, 0, 0) for z in range(1, dp)]
    if flat:
        in_dp = [(z, x, y) for z in range(1, dp) for x in range(phase) for y in range(ctx)]

    loads = [
        pltpu.make_async_copy(src, dst, load_sem.at[i])
        for i, (src, dst) in enumerate(
            [(k_hbm, kv), (seg_hbm, segv), (v_hbm, vv), (q_hbm, qv), (span_hbm, spanv), (read_hbm, readv)]
        )
    ]
    for load in loads:
        load.start()

    barrier = pltpu.get_barrier_semaphore()
    for by in in_dp[::-1] + in_group:
        pl.semaphore_signal(barrier, inc=1, device_id=away(*by), device_id_type=MESH)

    for step in range(1, steps + 1):

        @pl.when(here < step)
        def _():
            kr[step - 1] = jnp.zeros((tok, head_dim), kr.dtype)
            vr[step - 1] = jnp.zeros((tok, head_dim), vr.dtype)
            sr[step - 1] = jnp.full((1, tok), -1, jnp.int32)

    for load in loads[:3]:
        load.wait()
    pl.semaphore_wait(barrier, len(in_group) + len(in_dp))

    def halo(step):
        i = step - 1
        target = {"dp": at_dp, "phase": at_phase, "ctx": lax.rem(here + step, ctx)}
        return [
            pltpu.make_async_remote_copy(
                src_ref=src, dst_ref=dst.at[i], send_sem=ss.at[i], recv_sem=rs.at[i],
                device_id=target, device_id_type=MESH,
            )
            for src, dst, ss, rs in (
                (segv, sr, ssend, srecv), (kv, kr, ksend, krecv), (vv, vr, vsend, vrecv)
            )
        ]

    for step in range(1, steps + 1):

        @pl.when(here + step < ctx)
        def _():
            for copy in halo(step):
                copy.start()

    loads[3].wait()

    def query(h):
        return qv[:, h * head_dim:(h + 1) * head_dim]

    for h in range(heads):
        near[h] = lax.dot_general(kv[...], query(h), NT, preferred_element_type=jnp.float32)

    for load in loads[4:]:
        load.wait()

    qseg = segv[...].astype(jnp.float32)

    def down(row):
        wide = jnp.broadcast_to(row, (head_dim, tok))
        tall = jnp.transpose(wide)
        return jnp.concatenate([tall] * (tok // head_dim), axis=1)

    own_seg = down(qseg)
    vt_own = jnp.transpose(vv[...])
    reads = jnp.transpose(readv[...])
    tri = lax.broadcasted_iota(jnp.int32, (tok, tok), 0) <= lax.broadcasted_iota(jnp.int32, (tok, tok), 1)

    for step in range(1, steps + 1):

        @pl.when(here >= step)
        def _():
            for copy in halo(step)[:2]:
                copy.wait_recv()

    for step in range(1, steps + 1):
        far = down(sr[step - 1].astype(jnp.float32))
        if step == steps:
            far = jnp.where(tri, own_seg, far)
        bias[step - 1] = jnp.where(far == qseg, 0.0, OFF)

    rate = math.log2(math.e) / math.sqrt(head_dim)
    totals = []
    for h in range(heads):
        qh = query(h)
        scores = []
        for s in range(steps):
            sc = lax.dot_general(kr[s], qh, NT, preferred_element_type=jnp.float32)
            if s == steps - 1:
                sc = jnp.where(tri, near[h], sc)
            scores.append(sc + bias[s])
        top = functools.reduce(jnp.maximum, [jnp.max(sc, axis=0, keepdims=True) for sc in scores])
        probs = [jnp.exp2((sc - top) * rate) for sc in scores]
        totals.append(sum(jnp.sum(p, axis=0, keepdims=True) for p in probs))
        for s in range(steps):
            p = probs[s] if s < steps - 1 else jnp.where(tri, 0.0, probs[s])
            wts[h, s] = p.astype(jnp.bfloat16)
        wts[h, steps] = jnp.where(tri, probs[-1], 0.0).astype(jnp.bfloat16)

    for step in range(1, steps + 1):

        @pl.when(here >= step)
        def _():
            halo(step)[2].wait_recv()

    vts = [jnp.transpose(vr[s]) for s in range(steps)] + [vt_own]
    held = jnp.zeros((head_dim, tok), jnp.float32)
    for h in range(heads):
        acc = sum(
            lax.dot_general(vts[s], wts[h, s], NN, preferred_element_type=jnp.float32) for s in range(steps + 1)
        )
        full = acc / totals[h]
        held += full * reads[:, h:h + 1]
        near[h, :head_dim] = full

    score = jnp.sum(held, axis=0, keepdims=True)
    spans = spanv[...]
    lane = lax.broadcasted_iota(jnp.int32, (1, 128), 1)
    chosen = jnp.sum(jnp.where(spans == 1, score, 0.0), axis=1, keepdims=True)
    reject = jnp.sum(jnp.where(spans == 2, score, 0.0), axis=1, keepdims=True)
    row = jnp.where(lane == 0, chosen, jnp.where(lane == 1, reject, 0.0))

    def spread(slots, slot, targets, send_sem, recv_sem, between=lambda: None):
        for by in targets:
            pltpu.make_async_remote_copy(
                src_ref=slots.at[slot], dst_ref=slots.at[slot], send_sem=send_sem, recv_sem=recv_sem,
                device_id=away(*by), device_id_type=MESH,
            ).start()
        between()
        rest = slots.at[pl.ds(0, len(targets))]
        pltpu.make_async_copy(rest, rest, recv_sem).wait()
        return pltpu.make_async_copy(rest, rest, send_sem)

    def write():
        for h in range(heads):
            att_ref[:, h * head_dim:(h + 1) * head_dim] = jnp.transpose(near[h, :head_dim]).astype(att_ref.dtype)

    if flat:
        slot = at_dp * group + mine
        sums[slot] = row
        sent = [spread(sums, slot, in_dp[::-1] + in_group, asend, arecv, write)]
        for z in range(dp):
            tot_ref[z] = jnp.sum(sums[z * group:(z + 1) * group], axis=0) / 64.0
    else:
        sums[mine] = row
        sent = [spread(sums, mine, in_group, asend, arecv, write)]
        terms[at_dp] = jnp.sum(sums[...], axis=0) / 64.0
        sent.append(spread(terms, at_dp, in_dp, bsend, brecv))
        tot_ref[...] = terms[...]
    for copy in sent:
        copy.wait()
    for step in range(1, steps + 1):

        @pl.when(here + step < ctx)
        def _():
            for copy in halo(step):
                copy.wait_send()


def finish(att_ref, tot_ref, out_ref, spans_ref, loss_ref, sem):
    copy = pltpu.make_async_copy(att_ref, out_ref, sem)
    copy.start()
    tot = tot_ref[...]
    gap = tot[:, :, 1:2] - tot[:, :, 0:1]
    term = jnp.maximum(gap, 0.0) + jnp.log1p(jnp.exp(-jnp.abs(gap)))
    loss_ref[...] = jnp.sum(term, axis=0) / tot.shape[0]
    spans_ref[...] = tot_ref[lax.axis_index("dp")][:, :2]
    copy.wait()


def solution(mesh):
    dp, phase, ctx = mesh.shape["dp"], mesh.shape["phase"], mesh.shape["ctx"]
    steps = ctx // 4
    flat = dp * phase * ctx <= 64

    def per_device(queries, keys, values, segment_ids, span_ids, readout):
        tok, head_dim = keys.shape[1:]
        width = queries.shape[2]
        heads = width // head_dim
        any_spec = pl.BlockSpec(memory_space=pl.ANY)
        slots = dp * phase * ctx if flat else phase * ctx
        vmem = pl.BlockSpec(memory_space=pltpu.VMEM)
        dma = pltpu.SemaphoreType.DMA
        att, tot = pl.pallas_call(
            functools.partial(fused, (dp, phase, ctx, steps, flat)),
            out_shape=(
                jax.ShapeDtypeStruct((tok, width), jnp.bfloat16),
                jax.ShapeDtypeStruct((dp, 1, 128), jnp.float32),
            ),
            in_specs=[any_spec] * 6,
            out_specs=(vmem, vmem),
            scratch_shapes=[
                pltpu.VMEM((tok, width), jnp.bfloat16),
                pltpu.VMEM((tok, head_dim), jnp.bfloat16),
                pltpu.VMEM((tok, head_dim), jnp.bfloat16),
                pltpu.VMEM((1, tok), jnp.int32),
                pltpu.VMEM((1, tok), jnp.int32),
                pltpu.VMEM((heads, head_dim), jnp.float32),
                pltpu.VMEM((steps, tok, head_dim), jnp.bfloat16),
                pltpu.VMEM((steps, tok, head_dim), jnp.bfloat16),
                pltpu.VMEM((steps, 1, tok), jnp.int32),
                pltpu.VMEM((heads, tok, tok), jnp.float32),
                pltpu.VMEM((steps, tok, tok), jnp.float32),
                pltpu.VMEM((heads, steps + 1, tok, tok), jnp.bfloat16),
                pltpu.VMEM((slots, 1, 128), jnp.float32),
                pltpu.VMEM((dp, 1, 128), jnp.float32),
                dma((6,)),
                dma((steps,)), dma((steps,)), dma((steps,)),
                dma((steps,)), dma((steps,)), dma((steps,)),
                dma, dma, dma, dma,
            ],
            compiler_params=pltpu.CompilerParams(
                collective_id=0, has_side_effects=True, vmem_limit_bytes=32 * 1024 * 1024
            ),
            cost_estimate=pl.CostEstimate(
                flops=8 * heads * tok * tok * head_dim, bytes_accessed=4 * tok * width + 4 * tok * head_dim,
                transcendentals=heads * tok * tok,
            ),
        )(*[
            pltpu.with_memory_space_constraint(a, pltpu.HBM)
            for a in (queries[0], keys[0], values[0], segment_ids, span_ids, readout.reshape(heads, head_dim))
        ])
        att, spans, loss = pl.pallas_call(
            finish,
            out_shape=(
                jax.ShapeDtypeStruct((tok, width), jnp.bfloat16),
                jax.ShapeDtypeStruct((1, 2), jnp.float32),
                jax.ShapeDtypeStruct((1, 1), jnp.float32),
            ),
            in_specs=[any_spec, vmem],
            out_specs=(any_spec, vmem, vmem),
            scratch_shapes=[dma],
            compiler_params=pltpu.CompilerParams(vmem_limit_bytes=1024 * 1024),
        )(att, tot)
        return att[None], spans, loss.reshape(())

    in_specs = (
        P("dp", "ctx", "phase"),
        P("dp", "ctx", "phase"),
        P("dp", "ctx", "phase"),
        P("dp", "ctx"),
        P("dp", "ctx"),
        P("phase"),
    )
    out_specs = (P("dp", "ctx", "phase"), P("dp", None), P())
    return jax.shard_map(
        per_device, mesh=mesh, in_specs=in_specs, out_specs=out_specs, check_vma=False
    )
```
